32 devices in a mesh: expert: 8 (over z, y), tensor: 4 (over x, core).
Axes of the slice: x: 2, y: 2, z: 4, core: 2. Of those that a mesh axis runs over, the one named last changes fastest.
Arguments:
- hidden_in: bfloat16 [4096, 4096], P(('expert', 'tensor')), may hold values from -20 to 20
- context: bfloat16 [4096, 4096], P('expert', 'tensor'), may hold values from -6 to 6
- w_out: bfloat16 [4096, 4096], P('tensor', 'expert'), may hold values from -0.09375 to 0.09375
- norm_gain: float32 [4096], replicated, may hold values from 0.25 to 1.75
- expert_ids: int32 [4096, 8], P(('expert', 'tensor')), may hold values from 0 to 31, all different within a row; in each aligned block of 128 rows (0 to 127, 128 to 255, ...) at most 36 rows name the same one
- route_weight: float32 [4096, 8], P(('expert', 'tensor')), may hold values from 0.05 to 1
- w_gate_up: bfloat16 [32, 4096, 1536], P(('expert', 'tensor')), may hold values from -0.09375 to 0.09375
- w_down: bfloat16 [32, 768, 4096], P(('expert', 'tensor')), may hold values from -0.21875 to 0.21875
Outputs:
- attended: bfloat16 [4096, 4096], P(('expert', 'tensor'))
- mixed: bfloat16 [4096, 4096], P(('expert', 'tensor'))
The draws below stay inside these ranges and needn't reach their ends.
Inputs may be any that keep to these rules, and one draw needn't show every extreme that they name: `expert_ids`: each row names 8 different experts. Among the 128 rows of one device no expert is named more than 36 times, and in every draw some expert is named exactly 36 times by the rows of some device.
All inputs are finite; a program needn't handle non-finite values.
Results may differ from the reference program's by a relative error of at most 0.0053.
Values may be sent and summed in bfloat16 or wider, within the bound.
No kernel may reach another device: no remote copies, remote signals or barrier semaphores. Data moves between devices by JAX's collectives and lax.ppermute only.
A program may use at most 128 MiB of HBM per device.

```python
import math
import jax
import jax.numpy as jnp
import numpy as np
from jax import lax

D = 4096
HQ = 32
HD = 128
FF = 768
TOP_K = 8
TOK_DEV = 128
EXPERTS = 32
CAPACITY = 36
TOKENS = 4096
N_EXPERT = 8
N_TENSOR = 4


def draw_hidden_in(key, part):
    row_key, column_key, value_key = jax.random.split(key, 3)
    row_scale = jnp.exp(jax.random.uniform(row_key, (TOKENS, 1), jnp.float32) * math.log(10.0))
    column_scale = jnp.exp(jax.random.uniform(column_key, (1, D), jnp.float32) * math.log(10.0))
    values = jnp.clip(jax.random.normal(value_key, (TOKENS, D), jnp.float32), -4.0, 4.0)
    return (0.05 * values * row_scale * column_scale).astype(jnp.bfloat16)


def block_levels(rng, dims, cuts, smallest, largest):
    level = 1.0
    for position, parts in cuts:
        draws = jax.random.uniform(jax.random.fold_in(jax.random.fold_in(rng, 6), position), (parts,), jnp.float32, smallest / len(cuts), largest / len(cuts))
        level = level * jnp.repeat(jnp.exp(draws), dims[position] // parts).reshape((-1,) + (1,) * (len(dims) - 1 - position))
    return level


def deal_out(stream_key, own, number, rows, number_of, top, most, skew):
    ranking = jax.random.permutation(stream_key, number_of)
    crowded, usual = shares(number_of, rows * top, most, skew, True), shares(number_of, rows * top, most, skew, False)
    places = jnp.arange(number_of)

    def named(sizes, rotation):
        used = int((sizes > 0).sum())
        fixed = max(1, used // 4)
        moved = fixed + (places - fixed + rotation * (used - fixed)) % max(1, number_of - fixed)
        return jnp.zeros((number_of,), jnp.int32).at[ranking[jnp.where(places < fixed, places, moved)]].set(jnp.asarray(sizes, jnp.int32))

    sizes = jnp.where(number % 4 == 0, named(crowded, number // 4), named(usual, number - number // 4 - 1))
    mixed = jax.random.permutation(jax.random.fold_in(own, 3), number_of)
    giver, receiver = mixed[0:number_of // 2 * 2:2], mixed[1:number_of // 2 * 2:2]
    room = jnp.minimum(sizes[giver] - 1, most - sizes[receiver]) // 2
    room = jnp.where((giver == ranking[0]) | (receiver == ranking[0]) | (sizes[receiver] == 0), 0, jnp.maximum(room, 0))
    moved = jax.random.randint(jax.random.fold_in(own, 4), (number_of // 2,), 0, 1 << 20) % (room + 1)
    sizes = sizes.at[giver].add(-moved).at[receiver].add(moved)
    members = jnp.searchsorted(jnp.cumsum(sizes), jnp.arange(rows * top), side="right").astype(jnp.int32)
    table = members.reshape(top, rows).T
    table = table[jax.random.permutation(jax.random.fold_in(own, 1), rows)]
    rotation = jax.random.randint(jax.random.fold_in(own, 2), (rows, 1), 0, top)
    return jnp.take_along_axis(table, (jnp.arange(top)[None, :] + rotation) % top, axis=1)


def shares(count, total, reach, lean, full):
    weights = [(1 << 20) // math.isqrt(standing ** lean) + 1 for standing in range(1, count + 1)]
    largest = reach if full else min(reach, max(-(-total // count), total * weights[0] // sum(weights)))
    least = 1 if total - largest >= count - 1 else 0
    given, rest = [largest] + [least] * (count - 1), total - largest - least * (count - 1)
    while rest > 0:
        movable = [i for i in range(1, count) if given[i] < largest] or [i for i in range(1, count) if given[i] < reach]
        whole, left = sum([weights[i] for i in movable]), rest
        for i in movable:
            more = min(reach - given[i], max(1, left * weights[i] // whole), rest)
            given[i] = given[i] + more
            rest = rest - more
    return np.array(given)


def normal_values(stream_key, shape, scale, most, cuts=(), kind=jnp.bfloat16):
    array = jax.random.normal(stream_key, shape, jnp.float32) * scale
    if len(cuts) > 0:
        array = block_levels(stream_key, shape, cuts, -0.22, 0.18) * array
    return jnp.clip(array, min=-most, max=most).astype(kind)


def setup_inputs(seed: int = 0) -> dict:
    keys = jax.random.split(jax.random.key(seed), 9)
    hidden_in = draw_hidden_in(jax.random.fold_in(keys[8], 71), 0)
    context = normal_values(keys[1], (TOKENS, HQ * HD), 1.0, 6.0, ((0, 8), (1, 4)))
    w_out = normal_values(keys[2], (HQ * HD, D), (HQ * HD) ** -0.5, 0.09375, ((0, 4), (1, 8)))
    norm_gain = jnp.clip(1.0 + 0.15 * jax.random.normal(keys[3], (D,), jnp.float32), 0.25, 1.75)
    expert_ids_keys = jax.random.split(jax.random.fold_in(keys[4], 1), TOKENS // TOK_DEV)
    expert_ids_turns = jax.random.permutation(jax.random.fold_in(keys[4], 3), TOKENS // TOK_DEV)
    expert_ids = jax.vmap(lambda own, number: deal_out(jax.random.fold_in(keys[4], 2), own, number, TOK_DEV, EXPERTS, TOP_K, CAPACITY, 2))(expert_ids_keys, expert_ids_turns).reshape((TOKENS, TOP_K))
    route_weight = jnp.clip(jnp.exp(math.log(1.0) - 2.9957323 * jax.random.uniform(keys[5], (TOKENS, TOP_K), jnp.float32) ** block_levels(keys[5], (TOKENS, TOP_K), ((0, 32),), -0.2, 0.2)), 0.05, 1.0)
    w_gate_up = normal_values(keys[6], (EXPERTS, D, 2 * FF), D ** -0.5, 0.09375, ((0, 32),))
    w_down = normal_values(keys[7], (EXPERTS, FF, D), FF ** -0.5, 0.21875, ((0, 32),))
    return dict(hidden_in=hidden_in, context=context, w_out=w_out, norm_gain=norm_gain, expert_ids=expert_ids, route_weight=route_weight, w_gate_up=w_gate_up, w_down=w_down)


def slot_positions(expert_ids, devices):
    chosen = expert_ids.reshape(devices, -1)
    onehot = (chosen[:, :, None] == jnp.arange(EXPERTS, dtype=jnp.int32)[None, None, :]).astype(jnp.int32)
    before = jnp.cumsum(onehot, axis=1) - onehot
    return (chosen, lax.optimization_barrier(jnp.sum(before * onehot, axis=2)).astype(jnp.int32))

def reference(hidden_in, context, w_out, norm_gain, expert_ids, route_weight, w_gate_up, w_down):
    projected = jnp.dot(context, w_out, preferred_element_type=jnp.float32)
    residual = hidden_in.astype(jnp.float32) + projected
    attended = residual.astype(jnp.bfloat16)
    inverse = lax.rsqrt(lax.optimization_barrier(jnp.mean(residual * residual, axis=1, keepdims=True)) + 1e-06)
    normed = (residual * inverse * norm_gain[None, :]).astype(jnp.bfloat16)
    devices = N_EXPERT * N_TENSOR
    chosen, slots = slot_positions(expert_ids, devices)
    device_of = jnp.broadcast_to(jnp.arange(devices, dtype=jnp.int32)[:, None], chosen.shape)
    token_of = jnp.broadcast_to(jnp.arange(TOKENS, dtype=jnp.int32)[:, None], (TOKENS, TOP_K)).reshape(devices, -1)
    table = jnp.full((EXPERTS, devices, CAPACITY), TOKENS, jnp.int32).at[chosen, device_of, slots].set(token_of)
    weights = jnp.zeros((EXPERTS, devices, CAPACITY), jnp.float32).at[chosen, device_of, slots].set(route_weight.reshape(devices, -1))

    def one_expert(carry, inputs):
        token_index, row_weight, gate_up, down_proj = inputs
        gathered = jnp.take(normed, token_index, axis=0, mode='fill', fill_value=0)
        gate_and_up = jnp.dot(gathered, gate_up, preferred_element_type=jnp.float32)
        activated = (jax.nn.silu(gate_and_up[:, :FF]) * gate_and_up[:, FF:]).astype(jnp.bfloat16)
        result = jnp.dot(activated, down_proj, preferred_element_type=jnp.float32).astype(jnp.bfloat16)
        carry = carry.at[token_index].add(row_weight[:, None] * result.astype(jnp.float32), mode='drop')
        return (carry, None)
    moe_sum, _ = lax.scan(one_expert, jnp.zeros((TOKENS, D), jnp.float32), (table.reshape(EXPERTS, -1), weights.reshape(EXPERTS, -1), w_gate_up, w_down))
    mixed = (residual + moe_sum).astype(jnp.bfloat16)
    return (attended, mixed)
```

```python
import jax
import jax.numpy as jnp
from jax import lax
from jax.sharding import Mesh, PartitionSpec as P

SWAP = [(0, 1), (1, 0)]


def swap(array, axis):
    return lax.ppermute(array, axis, SWAP)


def dot(a, b):
    return jnp.dot(a, b, preferred_element_type=jnp.float32)


def after(array, *others):
    return lax.optimization_barrier((array, *others))[0]


def plane_order(planes):
    order = []
    for plane in range(planes):
        hops = [s - plane for s in range(planes) if s != plane]
        order.append(sorted(hops, key=lambda hop: (abs(hop), hop * (-1) ** plane)))
    return order


class PlaneGather:
    def __init__(self, block, zi):
        self.planes = lax.axis_size("outer")
        self.order = plane_order(self.planes)
        self.zi, self.hop = zi, 0
        self.up = self.down = block
        self.came, self.blocks = {}, [block]

    def start(self):
        self.hop += 1
        hop, planes = self.hop, self.planes
        self.up = lax.ppermute(self.up, "outer", [(i, i + 1) for i in range(hop - 1, planes - 1)])
        self.down = lax.ppermute(
            self.down, "outer", [(i, i - 1) for i in range(1, planes - hop + 1)]
        )

    def finish(self, *others):
        self.up, self.down, *_ = lax.optimization_barrier((self.up, self.down, *others))
        self.came[-self.hop], self.came[self.hop] = self.up, self.down
        hops = [self.order[plane][self.hop - 1] for plane in range(self.planes)]
        chosen = None
        for hop in sorted(set(hops)):
            if chosen is None:
                chosen = self.came[hop]
            else:
                here = jnp.zeros((), bool)
                for plane in range(self.planes):
                    if hops[plane] == hop:
                        here = here | (self.zi == plane)
                chosen = jnp.where(here, self.came[hop], chosen)
        self.blocks.append(chosen)


def project(context, w_out, expert_ids, route_weight, spots, make_tables):
    zi, yi, xi, ci = spots
    planes = lax.axis_size("outer")
    rows, depth = context.shape
    tok_count = rows // 4
    columns = PlaneGather(w_out, zi)
    columns.start()
    other_rows = swap(context, "inner")
    table = jnp.concatenate([expert_ids.astype(jnp.float32), route_weight], axis=1)
    table = jnp.stack([table, swap(table, "core")])
    table = PlaneGather(jnp.stack([table, swap(table, "pair")]), zi)
    table.start()
    parts, crossing = [], []
    for step in range(planes):
        if step:
            gate = (crossing[step - 2],) if step > 1 else ()
            columns.finish(*gate)
            table.finish(columns.up)
            if step + 1 < planes:
                columns.start()
                table.start()
        if step == 0:
            both = jnp.stack([context, other_rows]).reshape(2, 2, 2, tok_count, depth)
            theirs = lax.dynamic_index_in_dim(both, 1 - ci, 2, keepdims=False).reshape(-1, depth)
            mine = lax.dynamic_index_in_dim(both, ci, 2, keepdims=False).reshape(-1, depth)
        weights = columns.blocks[step]
        sent = dot(theirs, weights).astype(jnp.bfloat16)
        kept = dot(mine, weights) + swap(sent, "core").astype(jnp.float32)
        kept = kept.reshape(2, 2, tok_count, -1)
        sent = lax.dynamic_index_in_dim(kept, 1 - xi, 1, keepdims=False).astype(jnp.bfloat16)
        crossing.append(sent)
        kept = lax.dynamic_index_in_dim(kept, xi, 1, keepdims=False)
        kept = kept + swap(sent, "pair").astype(jnp.float32)
        other = swap(kept[1].astype(jnp.bfloat16), "inner").astype(jnp.float32)
        low = jnp.where(yi == 0, kept[0], other)
        high = jnp.where(yi == 0, other, kept[0])
        parts.append(jnp.concatenate([low, high], axis=1))
    order = jnp.array(
        [
            [([0] + hops).index(target - plane) for target in range(planes)]
            for plane, hops in enumerate(plane_order(planes))
        ]
    )[zi]
    parts = jnp.stack(parts)
    projected = jnp.concatenate(
        [lax.dynamic_index_in_dim(parts, order[p], 0, keepdims=False) for p in range(planes)], axis=1
    )
    return projected, make_tables(jnp.stack(table.blocks))


def routes(expert_ids, route_weight, expert, capacity, rounds):
    devices, tok_count, _ = expert_ids.shape
    named = expert_ids == expert
    chosen = jnp.any(named, axis=2)
    weight = jnp.sum(jnp.where(named, route_weight, 0.0), axis=2)
    earlier = jnp.arange(tok_count)[:, None] < jnp.arange(tok_count)[None, :]
    slots = dot(chosen.astype(jnp.bfloat16), earlier.astype(jnp.bfloat16)).astype(jnp.int32)
    first = jnp.arange(devices) % (devices // rounds) * capacity
    row = jnp.where(chosen, slots + first[:, None], -1)
    return row.reshape(rounds, -1), weight.reshape(rounds, -1)


def routing_tables(table, spots, capacity, rounds):
    zi, yi, xi, ci = spots
    planes, tok_count, top_count = table.shape[0], table.shape[-2], table.shape[-1] // 2
    group = planes // rounds
    rows = group * 4 * capacity
    table = table.reshape(rounds, group, 4, tok_count, -1).swapaxes(1, 2)
    table = table.reshape(planes * 4, tok_count, -1)
    pick, place = [], []
    for side in range(2):
        expert = ((zi * 2 + (yi ^ side)) * 2 + xi) * 2 + ci
        row, weight = routes(
            table[..., :top_count],
            table[..., top_count:],
            expert.astype(jnp.float32),
            capacity,
            rounds,
        )
        pick.append((row[:, None, :] == jnp.arange(rows)[None, :, None]).astype(jnp.bfloat16))
        spread = jnp.where(row[:, :, None] == jnp.arange(rows), weight[:, :, None], 0.0)
        high = spread.astype(jnp.bfloat16)
        low = (spread - high.astype(jnp.float32)).astype(jnp.bfloat16)
        place += [high, low]
    place = jnp.concatenate(place, axis=2).reshape(rounds, 2, 2, group * tok_count, -1)
    return lax.optimization_barrier((*pick, place[:, :, 0], place[:, :, 1]))


def scatter_planes(pieces, zi):
    planes = lax.axis_size("outer")
    order = plane_order(planes)

    def piece(hop):
        chosen = None
        for step in range(planes - 1):
            here = [plane for plane in range(planes) if order[plane][step] == hop]
            if not here:
                continue
            if chosen is None:
                chosen = pieces[step + 1]
            else:
                at = jnp.zeros((), bool)
                for plane in here:
                    at = at | (zi == plane)
                chosen = jnp.where(at, pieces[step + 1], chosen)
        return chosen

    up = down = None
    for hop in range(planes - 1, 0, -1):
        up = piece(hop) if up is None else piece(hop) + up.astype(jnp.float32)
        down = piece(-hop) if down is None else piece(-hop) + down.astype(jnp.float32)
        up = lax.ppermute(
            up.astype(jnp.bfloat16), "outer", [(i, i + 1) for i in range(planes - hop)]
        )
        down = lax.ppermute(
            down.astype(jnp.bfloat16), "outer", [(i, i - 1) for i in range(hop, planes)]
        )
    return up.astype(jnp.float32) + down.astype(jnp.float32)


def on_device(hidden_in, context, w_out, norm_gain, expert_ids, route_weight, w_gate_up, w_down):
    tok_count, width = hidden_in.shape
    hidden_units = w_down.shape[1]
    planes = lax.axis_size("outer")
    zi, yi = lax.axis_index("outer"), lax.axis_index("inner")
    xi, ci = lax.axis_index("pair"), lax.axis_index("core")
    capacity = tok_count * expert_ids.shape[1] * 9 // (8 * planes * 8)
    rounds = min(planes, 8)
    group = planes // rounds
    rows = group * 4 * capacity
    held = group * tok_count

    spots = (zi, yi, xi, ci)
    projected, tables = project(
        context,
        w_out,
        expert_ids,
        route_weight,
        spots,
        lambda table: routing_tables(table, spots, capacity, rounds),
    )
    pick_ours, pick_theirs, place_kept, place_sent = tables
    residual = hidden_in.astype(jnp.float32) + projected
    attended = residual.astype(jnp.bfloat16)
    inverse = lax.rsqrt(jnp.mean(residual * residual, axis=1, keepdims=True) + 1e-06)
    normed = (residual * inverse * norm_gain[None, :]).astype(jnp.bfloat16)

    gather = PlaneGather(normed, zi)
    across = [None] * rounds
    ours, leaving, out = [None] * rounds, [None] * rounds, [None] * rounds

    def round_block(step):
        if step == 0 and planes > 1:
            gather.start()
        while len(gather.blocks) < (step + 1) * group:
            ahead = len(gather.blocks) // group - 2
            gather.finish(*([leaving[ahead]] if ahead >= 0 else []))
            if len(gather.blocks) < planes:
                gather.start()
        blocks = gather.blocks[step * group : (step + 1) * group]
        return blocks[0] if group == 1 else jnp.concatenate(blocks)

    def pick_rows(step):
        block = round_block(step)
        if step:
            block = after(block, across[step - 1])
        across[step] = swap(block, "pair")
        tokens = jnp.concatenate(
            [block, swap(block, "core"), across[step], swap(across[step], "core")]
        )
        leaving[step] = dot(pick_theirs[step], tokens).astype(jnp.bfloat16)
        ours[step] = dot(pick_ours[step], tokens).astype(jnp.bfloat16)

    def expert(step, *others):
        theirs = after(swap(leaving[step], "inner"), *others)
        gate_up = dot(jnp.concatenate([ours[step], theirs]), w_gate_up[0])
        act = jax.nn.silu(gate_up[:, :hidden_units]) * gate_up[:, hidden_units:]
        out[step] = dot(act.astype(jnp.bfloat16), w_down[0]).astype(jnp.bfloat16)

    pick_rows(0)
    for step in range(rounds):
        others = []
        if step + 1 < rounds:
            pick_rows(step + 1)
            others.append(leaving[step + 1])
        if step:
            others.append(out[step - 1])
        expert(step, *others)

    pieces = [None] * planes
    came = crossed = sent = None
    for step in range(rounds - 1, -1, -1):
        back = out[step][rows:]
        came = swap(back if came is None else after(back, came), "inner")
        back = came if sent is None else after(came, sent)
        results = jnp.concatenate([out[step][:rows]] * 2 + [back] * 2)
        sent = dot(place_sent[step].reshape(2 * held, -1), results).astype(jnp.bfloat16)
        kept = dot(place_kept[step].reshape(2 * held, -1), results)
        kept = (kept + swap(sent, "core").astype(jnp.float32)).reshape(2, held, width)
        sent = kept[1].astype(jnp.bfloat16)
        crossed = swap(sent if crossed is None else after(sent, crossed), "pair")
        part = (kept[0] + crossed.astype(jnp.float32)).reshape(group, tok_count, width)
        for j in range(group):
            pieces[step * group + j] = part[j]
    total = residual + pieces[0] + scatter_planes(pieces, zi)
    return attended, total.astype(jnp.bfloat16)


def solution(mesh):
    experts, tensors = mesh.shape["expert"], mesh.shape["tensor"]
    split = Mesh(
        mesh.devices.reshape(experts // 2, 2, tensors // 2, 2), ("outer", "inner", "pair", "core")
    )
    expert, tensor = ("outer", "inner"), ("pair", "core")
    every = expert + tensor
    in_specs = (
        P(every, None),
        P(expert, tensor),
        P(tensor, expert),
        P(),
        P(every, None),
        P(every, None),
        P(every, None, None),
        P(every, None, None),
    )
    out_specs = (P(every, None), P(every, None))
    return jax.shard_map(
        on_device, mesh=split, in_specs=in_specs, out_specs=out_specs, check_vma=False
    )
```

```python
import functools

import jax
import jax.numpy as jnp
from jax import lax
from jax.experimental import pallas as pl
from jax.experimental.pallas import tpu as pltpu
from jax.sharding import Mesh, PartitionSpec as P

SWAP = [(0, 1), (1, 0)]
LAG = 1


def swap(array, axis):
    return lax.ppermute(array, axis, SWAP)


def dot(a, b):
    return jnp.dot(a, b, preferred_element_type=jnp.float32)


def after(array, *others):
    return lax.optimization_barrier((array, *others))[0]


def plane_order(planes):
    order = []
    for plane in range(planes):
        hops = [s - plane for s in range(planes) if s != plane]
        order.append(sorted(hops, key=lambda hop: (abs(hop), hop * (-1) ** plane)))
    return order


class PlaneGather:
    def __init__(self, block, zi):
        self.planes = lax.axis_size("outer")
        self.order = plane_order(self.planes)
        self.zi, self.hop = zi, 0
        self.up = self.down = block
        self.came, self.blocks = {}, [block]

    def start(self):
        self.hop += 1
        hop, planes = self.hop, self.planes
        self.up = lax.ppermute(self.up, "outer", [(i, i + 1) for i in range(hop - 1, planes - 1)])
        self.down = lax.ppermute(
            self.down, "outer", [(i, i - 1) for i in range(1, planes - hop + 1)]
        )

    def finish(self, *others):
        self.up, self.down, *_ = lax.optimization_barrier((self.up, self.down, *others))
        self.came[-self.hop], self.came[self.hop] = self.up, self.down
        hops = [self.order[plane][self.hop - 1] for plane in range(self.planes)]
        chosen = None
        for hop in sorted(set(hops)):
            if chosen is None:
                chosen = self.came[hop]
            else:
                here = jnp.zeros((), bool)
                for plane in range(self.planes):
                    if hops[plane] == hop:
                        here = here | (self.zi == plane)
                chosen = jnp.where(here, self.came[hop], chosen)
        self.blocks.append(chosen)


def project(context, w_out, expert_ids, route_weight, spots, make_tables):
    zi, yi, xi, ci = spots
    planes = lax.axis_size("outer")
    rows, depth = context.shape
    tok_count = rows // 4
    columns = PlaneGather(w_out, zi)
    columns.start()
    other_rows = swap(context, "inner")
    table = jnp.concatenate([expert_ids.T.astype(jnp.float32), route_weight.T])
    table = jnp.stack([table, swap(table, "pair")])
    order = plane_order(planes)
    table = after(table, other_rows)
    by_offset = [table] + [
        lax.ppermute(table, "outer", [(i, i ^ offset) for i in range(planes)])
        for offset in range(1, planes)
    ]
    near = [[plane ^ (plane + hop) for hop in [0] + order[plane]] for plane in range(planes)]
    tables = make_tables(jnp.take(jnp.stack(by_offset), jnp.array(near)[zi], axis=0))
    both = jnp.stack([context, other_rows]).reshape(2, 2, 2, tok_count, depth)
    theirs = lax.dynamic_index_in_dim(both, 1 - ci, 2, keepdims=False).reshape(-1, depth)
    mine = lax.dynamic_index_in_dim(both, ci, 2, keepdims=False).reshape(-1, depth)
    parts, crossing = [], []
    for step in range(planes):
        if step:
            gates = list(crossing[:2] if step == 2 else crossing[step - 1 :] if step > 2 else [])
            if step == min(2, planes - 1):
                gates += tables
            columns.finish(*gates)
            if step + 1 < planes:
                columns.start()
        weights = columns.blocks[step]
        sent = dot(theirs, weights).astype(jnp.bfloat16)
        kept = dot(mine, weights) + swap(sent, "core").astype(jnp.float32)
        kept = kept.reshape(2, 2, tok_count, -1)
        sent = lax.dynamic_index_in_dim(kept, 1 - xi, 1, keepdims=False).astype(jnp.bfloat16)
        crossing.append(sent)
        kept = lax.dynamic_index_in_dim(kept, xi, 1, keepdims=False)
        kept = kept + swap(sent, "pair").astype(jnp.float32)
        other = swap(kept[1].astype(jnp.bfloat16), "inner").astype(jnp.float32)
        low = jnp.where(yi == 0, kept[0], other)
        high = jnp.where(yi == 0, other, kept[0])
        parts.append(jnp.concatenate([low, high], axis=1))
    where = [
        [([0] + order[plane]).index(target - plane) for target in range(planes)]
        for plane in range(planes)
    ]
    where = jnp.array(where)[zi]
    parts = jnp.stack(parts)
    projected = jnp.concatenate(
        [lax.dynamic_index_in_dim(parts, where[p], 0, keepdims=False) for p in range(planes)], axis=1
    )
    return projected, tables


def routing_tables(table, spots, capacity, rounds):
    zi, yi, xi, ci = spots
    planes, _, top_count, tok_count = table.shape
    top_count //= 2
    group = planes // rounds
    rows = group * capacity
    table = table.reshape(rounds, group, 2, -1, tok_count)
    chosen, weight = [], []
    for core in range(2):
        for side in range(2):
            expert = ((zi * 2 + (yi ^ side)) * 2 + xi) * 2 + (ci ^ core)
            named = table[..., :top_count, :] == expert.astype(jnp.float32)
            chosen.append(jnp.any(named, axis=3))
            weight.append(jnp.sum(jnp.where(named, table[..., top_count:, :], 0.0), axis=3))
    chosen, weight = jnp.stack(chosen), jnp.stack(weight)
    earlier = jnp.arange(tok_count)[:, None] < jnp.arange(tok_count)[None, :]
    slots = dot(chosen.astype(jnp.bfloat16), earlier.astype(jnp.bfloat16)).astype(jnp.int32)
    first = jnp.arange(4)[:, None, None, None, None] * rows
    first = first + jnp.arange(group)[None, None, :, None, None] * capacity
    row = jnp.where(chosen, slots + first, -1)
    order = (3, 0, 1, 2, 4)
    row = row.transpose(order).reshape(2, 4, rounds, -1)
    weight = weight.transpose(order).reshape(2, 4, rounds, -1)
    parts = []
    for part in range(2):
        own, theirs, other, diagonal = (row[part, i, :, None, :] for i in range(4))
        spot = jnp.arange(2 * rows)[None, :, None]
        kept = (own == spot) | (theirs == spot)
        spot = spot + 2 * rows
        sent = (other == spot) | (diagonal == spot)
        spread = 0.0
        for i in range(4):
            here = row[part, i, :, :, None] == jnp.arange(4 * rows)
            spread = spread + jnp.where(here, weight[part, i, :, :, None], 0.0)
        high = spread.astype(jnp.bfloat16)
        low = (spread - high.astype(jnp.float32)).astype(jnp.bfloat16)
        parts += [kept.astype(jnp.bfloat16), sent.astype(jnp.bfloat16), high, low]
    return lax.optimization_barrier(tuple(parts))


def expert_kernel(steps, own, theirs, gate, up, down, own_out, theirs_out, tokens, total):
    step = pl.program_id(0)
    rows = own.shape[0]

    @pl.when(step == 0)
    def _():
        tokens[:rows, :] = own[...]
        tokens[rows:, :] = theirs[...]

    gated = dot(tokens[...], gate[0])
    act = gated / (1.0 + jnp.exp(-gated)) * dot(tokens[...], up[0])
    part = dot(act.astype(jnp.bfloat16), down[0])

    @pl.when(step == 0)
    def _():
        total[...] = part

    @pl.when(step > 0)
    def _():
        total[...] += part

    @pl.when(step == steps - 1)
    def _():
        own_out[...] = total[:rows, :].astype(jnp.bfloat16)
        theirs_out[...] = total[rows:, :].astype(jnp.bfloat16)


def expert_block(own, theirs, w_gate_up, w_down):
    rows, width = own.shape
    hidden_units = w_down.shape[1]
    tile = 256 if hidden_units % 256 == 0 else 128
    steps = hidden_units // tile
    whole = pl.BlockSpec((rows, width), lambda i: (0, 0))
    return pl.pallas_call(
        functools.partial(expert_kernel, steps),
        grid=(steps,),
        in_specs=[
            whole,
            whole,
            pl.BlockSpec((1, width, tile), lambda i: (0, 0, i)),
            pl.BlockSpec((1, width, tile), lambda i: (0, 0, i + steps)),
            pl.BlockSpec((1, tile, width), lambda i: (0, i, 0)),
        ],
        out_specs=[whole, whole],
        out_shape=[jax.ShapeDtypeStruct((rows, width), jnp.bfloat16)] * 2,
        scratch_shapes=[
            pltpu.VMEM((2 * rows, width), jnp.bfloat16),
            pltpu.VMEM((2 * rows, width), jnp.float32),
        ],
        compiler_params=pltpu.CompilerParams(vmem_limit_bytes=44 * 2**20),
        cost_estimate=pl.CostEstimate(flops=1, bytes_accessed=1, transcendentals=0),
    )(own, theirs, w_gate_up, w_gate_up, w_down)


def scatter_planes(pieces, zi):
    planes = lax.axis_size("outer")
    order = plane_order(planes)

    def piece(hop):
        chosen = None
        for step in range(planes - 1):
            here = [plane for plane in range(planes) if order[plane][step] == hop]
            if not here:
                continue
            if chosen is None:
                chosen = pieces[step + 1]
            else:
                at = jnp.zeros((), bool)
                for plane in here:
                    at = at | (zi == plane)
                chosen = jnp.where(at, pieces[step + 1], chosen)
        return chosen

    up = down = None
    for hop in range(planes - 1, 0, -1):
        up = piece(hop) if up is None else piece(hop) + up.astype(jnp.float32)
        down = piece(-hop) if down is None else piece(-hop) + down.astype(jnp.float32)
        up = lax.ppermute(
            up.astype(jnp.bfloat16), "outer", [(i, i + 1) for i in range(planes - hop)]
        )
        down = lax.ppermute(
            down.astype(jnp.bfloat16), "outer", [(i, i - 1) for i in range(hop, planes)]
        )
    return up.astype(jnp.float32) + down.astype(jnp.float32)


def on_device(hidden_in, context, w_out, norm_gain, expert_ids, route_weight, w_gate_up, w_down):
    tok_count, width = hidden_in.shape
    planes = lax.axis_size("outer")
    zi, yi = lax.axis_index("outer"), lax.axis_index("inner")
    xi, ci = lax.axis_index("pair"), lax.axis_index("core")
    capacity = tok_count * expert_ids.shape[1] * 9 // (8 * planes * 8)
    rounds = min(planes, 8)
    group = planes // rounds
    rows = group * capacity

    spots = (zi, yi, xi, ci)
    projected, tables = project(
        context,
        w_out,
        expert_ids,
        route_weight,
        spots,
        lambda table: routing_tables(table, spots, capacity, rounds),
    )
    parts = (tables[:4], tables[4:])
    residual = hidden_in.astype(jnp.float32) + projected
    attended = residual.astype(jnp.bfloat16)
    inverse = lax.rsqrt(jnp.mean(residual * residual, axis=1, keepdims=True) + 1e-06)
    normed = (residual * inverse * norm_gain[None, :]).astype(jnp.bfloat16)

    gather = PlaneGather(normed, zi)
    across, out = [None] * rounds, [None] * rounds
    leaving = [[None, None] for _ in range(rounds)]
    came = [[None, None] for _ in range(rounds)]
    ours = [[None, None] for _ in range(rounds)]
    line = []

    def round_block(step):
        if step == 0 and planes > 1:
            gather.start()
        while len(gather.blocks) < (step + 1) * group:
            ahead = len(gather.blocks) // group - (1 if group == 1 else 2)
            gather.finish(*([across[ahead]] if ahead >= 0 else []))
            if len(gather.blocks) < planes:
                gather.start()
        blocks = gather.blocks[step * group : (step + 1) * group]
        return blocks[0] if group == 1 else jnp.concatenate(blocks)

    def pick_rows(step, part, tokens):
        pick_kept, pick_sent = parts[part][0][step], parts[part][1][step]
        got = swap(dot(pick_sent, tokens).astype(jnp.bfloat16), "core")
        kept = dot(pick_kept, tokens).astype(jnp.bfloat16)
        got, kept, *_ = lax.optimization_barrier((got, kept, *line[-LAG : len(line) - LAG + 1]))
        ours[step][part] = [kept[:rows], got[:rows]]
        leaving[step][part] = jnp.concatenate([kept[rows:], got[rows:]])
        came[step][part] = swap(leaving[step][part], "inner")
        line.append(came[step][part])

    def expert(step):
        others = [out[step - 1][1]] if step else []
        if step + 1 < rounds:
            others.append(leaving[step + 1][1])
        theirs = jnp.concatenate(came[step])
        theirs = after(theirs, *others) if others else theirs
        own = jnp.concatenate(ours[step][0] + ours[step][1])
        out[step] = expert_block(own, theirs, w_gate_up, w_down)

    for step in range(rounds + 1):
        if step < rounds:
            block = round_block(step)
            across[step] = swap(block, "pair")
        if step:
            pick_rows(step - 1, 1, across[step - 1])
        if step < rounds:
            pick_rows(step, 0, block)
            across[step] = after(across[step], leaving[step][0])
        if step > 1:
            expert(step - 2)
            if step < rounds:
                across[step] = after(across[step], out[step - 2][1])
    expert(rounds - 1)

    pieces = [None] * planes
    line = []
    crossed = sent = None
    for step in range(rounds - 1, -1, -1):
        own, theirs = out[step]
        results = [None, None]
        for part in (1, 0):
            span = slice(2 * rows * part, 2 * rows * (part + 1))
            mine, back = own[span], theirs[span]
            others = line[-LAG : len(line) - LAG + 1]
            line.append(swap(after(back, *others) if others else back, "inner"))
            back = line[-1] if sent is None else after(line[-1], sent)
            got = swap(jnp.concatenate([mine[rows:], back[rows:]]), "core")
            results[part] = jnp.concatenate([mine[:rows], back[:rows], got])
            if part:
                if crossed is not None:
                    results[part] = after(results[part], crossed)
                high, low = parts[part][2][step], parts[part][3][step]
                sent = (dot(high, results[part]) + dot(low, results[part])).astype(jnp.bfloat16)
                crossed = swap(sent, "pair")
        high, low = parts[0][2][step], parts[0][3][step]
        piece = dot(high, results[0]) + dot(low, results[0]) + crossed.astype(jnp.float32)
        piece = piece.reshape(group, tok_count, width)
        for j in range(group):
            pieces[step * group + j] = piece[j]
    total = residual + pieces[0] + scatter_planes(pieces, zi)
    return attended, total.astype(jnp.bfloat16)


def solution(mesh):
    experts, tensors = mesh.shape["expert"], mesh.shape["tensor"]
    split = Mesh(
        mesh.devices.reshape(experts // 2, 2, tensors // 2, 2), ("outer", "inner", "pair", "core")
    )
    expert, tensor = ("outer", "inner"), ("pair", "core")
    every = expert + tensor
    in_specs = (
        P(every, None),
        P(expert, tensor),
        P(tensor, expert),
        P(),
        P(every, None),
        P(every, None),
        P(every, None, None),
        P(every, None, None),
    )
    out_specs = (P(every, None), P(every, None))
    return jax.shard_map(
        on_device, mesh=split, in_specs=in_specs, out_specs=out_specs, check_vma=False
    )
```

```python
import functools

import jax
import jax.numpy as jnp
from jax import lax
from jax.experimental import pallas as pl
from jax.experimental.pallas import tpu as pltpu
from jax.sharding import Mesh, PartitionSpec as P

SWAP = [(0, 1), (1, 0)]
LAG = 1


def swap(array, axis):
    return lax.ppermute(array, axis, SWAP)


def dot(a, b):
    return jnp.dot(a, b, preferred_element_type=jnp.float32)


def after(array, *others):
    return lax.optimization_barrier((array, *others))[0]


def plane_order(planes):
    order = []
    for plane in range(planes):
        hops = [s - plane for s in range(planes) if s != plane]
        order.append(sorted(hops, key=lambda hop: (abs(hop), hop * (-1) ** plane)))
    return order


class PlaneGather:
    def __init__(self, block, zi):
        self.planes = lax.axis_size("outer")
        self.order = plane_order(self.planes)
        self.zi, self.hop = zi, 0
        self.up = self.down = block
        self.came, self.blocks = {}, [block]

    def start(self):
        self.hop += 1
        hop, planes = self.hop, self.planes
        self.up = lax.ppermute(self.up, "outer", [(i, i + 1) for i in range(hop - 1, planes - 1)])
        self.down = lax.ppermute(
            self.down, "outer", [(i, i - 1) for i in range(1, planes - hop + 1)]
        )

    def finish(self, *others):
        self.up, self.down, *_ = lax.optimization_barrier((self.up, self.down, *others))
        self.came[-self.hop], self.came[self.hop] = self.up, self.down
        hops = [self.order[plane][self.hop - 1] for plane in range(self.planes)]
        chosen = None
        for hop in sorted(set(hops)):
            if chosen is None:
                chosen = self.came[hop]
            else:
                here = jnp.zeros((), bool)
                for plane in range(self.planes):
                    if hops[plane] == hop:
                        here = here | (self.zi == plane)
                chosen = jnp.where(here, self.came[hop], chosen)
        self.blocks.append(chosen)


def project(context, w_out, expert_ids, route_weight, spots, make_tables):
    zi, yi, xi, ci = spots
    planes = lax.axis_size("outer")
    rows, depth = context.shape
    tok_count = rows // 4
    columns = PlaneGather(w_out, zi)
    columns.start()
    other_rows = swap(context, "inner")
    table = jnp.concatenate([expert_ids.T.astype(jnp.float32), route_weight.T])
    table = jnp.stack([table, swap(table, "pair")])
    order = plane_order(planes)
    table = after(table, other_rows)
    by_offset = [table] + [
        lax.ppermute(table, "outer", [(i, i ^ offset) for i in range(planes)])
        for offset in range(1, planes)
    ]
    near = [[plane ^ (plane + hop) for hop in [0] + order[plane]] for plane in range(planes)]
    tables = make_tables(jnp.take(jnp.stack(by_offset), jnp.array(near)[zi], axis=0))
    both = jnp.stack([context, other_rows]).reshape(2, 2, 2, tok_count, depth)
    theirs = lax.dynamic_index_in_dim(both, 1 - ci, 2, keepdims=False).reshape(-1, depth)
    mine = lax.dynamic_index_in_dim(both, ci, 2, keepdims=False).reshape(-1, depth)
    parts, crossing = [], []
    for step in range(planes):
        if step:
            gates = list(crossing[:2] if step == 2 else crossing[step - 1 :] if step > 2 else [])
            if step == min(2, planes - 1):
                gates += tables
            columns.finish(*gates)
            if step + 1 < planes:
                columns.start()
        weights = columns.blocks[step]
        sent = dot(theirs, weights).astype(jnp.bfloat16)
        kept = dot(mine, weights) + swap(sent, "core").astype(jnp.float32)
        kept = kept.reshape(2, 2, tok_count, -1)
        sent = lax.dynamic_index_in_dim(kept, 1 - xi, 1, keepdims=False).astype(jnp.bfloat16)
        crossing.append(sent)
        kept = lax.dynamic_index_in_dim(kept, xi, 1, keepdims=False)
        kept = kept + swap(sent, "pair").astype(jnp.float32)
        other = swap(kept[1].astype(jnp.bfloat16), "inner").astype(jnp.float32)
        low = jnp.where(yi == 0, kept[0], other)
        high = jnp.where(yi == 0, other, kept[0])
        parts.append(jnp.concatenate([low, high], axis=1))
    where = [
        [([0] + order[plane]).index(target - plane) for target in range(planes)]
        for plane in range(planes)
    ]
    where = jnp.array(where)[zi]
    parts = jnp.stack(parts)
    projected = jnp.concatenate(
        [lax.dynamic_index_in_dim(parts, where[p], 0, keepdims=False) for p in range(planes)], axis=1
    )
    return projected, tables


def routing_tables(table, spots, capacity, rounds):
    zi, yi, xi, ci = spots
    planes, _, top_count, tok_count = table.shape
    top_count //= 2
    group = planes // rounds
    rows = group * capacity
    table = table.reshape(rounds, group, 2, -1, tok_count)
    chosen, weight = [], []
    for core in range(2):
        for side in range(2):
            expert = ((zi * 2 + (yi ^ side)) * 2 + xi) * 2 + (ci ^ core)
            named = table[..., :top_count, :] == expert.astype(jnp.float32)
            chosen.append(jnp.any(named, axis=3))
            weight.append(jnp.sum(jnp.where(named, table[..., top_count:, :], 0.0), axis=3))
    chosen, weight = jnp.stack(chosen), jnp.stack(weight)
    earlier = jnp.arange(tok_count)[:, None] < jnp.arange(tok_count)[None, :]
    slots = dot(chosen.astype(jnp.bfloat16), earlier.astype(jnp.bfloat16)).astype(jnp.int32)
    first = jnp.arange(4)[:, None, None, None, None] * rows
    first = first + jnp.arange(group)[None, None, :, None, None] * capacity
    row = jnp.where(chosen, slots + first, -1)
    order = (3, 0, 1, 2, 4)
    row = row.transpose(order).reshape(2, 4, rounds, -1)
    weight = weight.transpose(order).reshape(2, 4, rounds, -1)
    parts = []
    for part in range(2):
        own, theirs, other, diagonal = (row[part, i, :, None, :] for i in range(4))
        spot = jnp.arange(2 * rows)[None, :, None]
        kept = (own == spot) | (theirs == spot)
        spot = spot + 2 * rows
        sent = (other == spot) | (diagonal == spot)
        spread = 0.0
        for i in range(4):
            here = row[part, i, :, :, None] == jnp.arange(4 * rows)
            spread = spread + jnp.where(here, weight[part, i, :, :, None], 0.0)
        high = spread.astype(jnp.bfloat16)
        low = (spread - high.astype(jnp.float32)).astype(jnp.bfloat16)
        parts += [kept.astype(jnp.bfloat16), sent.astype(jnp.bfloat16), high, low]
    return lax.optimization_barrier(tuple(parts))


def expert_kernel(steps, own, theirs, gate, up, down, own_out, theirs_out, tokens, total):
    step = pl.program_id(0)
    rows = own.shape[0]

    @pl.when(step == 0)
    def _():
        tokens[:rows, :] = own[...]
        tokens[rows:, :] = theirs[...]

    gated = dot(tokens[...], gate[0])
    act = gated / (1.0 + jnp.exp(-gated)) * dot(tokens[...], up[0])
    part = dot(act.astype(jnp.bfloat16), down[0])

    @pl.when(step == 0)
    def _():
        total[...] = part

    @pl.when(step > 0)
    def _():
        total[...] += part

    @pl.when(step == steps - 1)
    def _():
        own_out[...] = total[:rows, :].astype(jnp.bfloat16)
        theirs_out[...] = total[rows:, :].astype(jnp.bfloat16)


def expert_block(own, theirs, w_gate_up, w_down):
    rows, width = own.shape
    hidden_units = w_down.shape[1]
    tile = 256 if hidden_units % 256 == 0 else 128
    steps = hidden_units // tile
    whole = pl.BlockSpec((rows, width), lambda i: (0, 0))
    return pl.pallas_call(
        functools.partial(expert_kernel, steps),
        grid=(steps,),
        in_specs=[
            whole,
            whole,
            pl.BlockSpec((1, width, tile), lambda i: (0, 0, i)),
            pl.BlockSpec((1, width, tile), lambda i: (0, 0, i + steps)),
            pl.BlockSpec((1, tile, width), lambda i: (0, i, 0)),
        ],
        out_specs=[whole, whole],
        out_shape=[jax.ShapeDtypeStruct((rows, width), jnp.bfloat16)] * 2,
        scratch_shapes=[
            pltpu.VMEM((2 * rows, width), jnp.bfloat16),
            pltpu.VMEM((2 * rows, width), jnp.float32),
        ],
        compiler_params=pltpu.CompilerParams(vmem_limit_bytes=44 * 2**20),
        cost_estimate=pl.CostEstimate(flops=1, bytes_accessed=1, transcendentals=0),
    )(own, theirs, w_gate_up, w_gate_up, w_down)


def scatter_planes(pieces, zi):
    planes = lax.axis_size("outer")
    order = plane_order(planes)

    def piece(hop):
        chosen = None
        for step in range(planes - 1):
            here = [plane for plane in range(planes) if order[plane][step] == hop]
            if not here:
                continue
            if chosen is None:
                chosen = pieces[step + 1]
            else:
                at = jnp.zeros((), bool)
                for plane in here:
                    at = at | (zi == plane)
                chosen = jnp.where(at, pieces[step + 1], chosen)
        return chosen

    up = down = None
    for hop in range(planes - 1, 0, -1):
        up = piece(hop) if up is None else piece(hop) + up.astype(jnp.float32)
        down = piece(-hop) if down is None else piece(-hop) + down.astype(jnp.float32)
        up = lax.ppermute(
            up.astype(jnp.bfloat16), "outer", [(i, i + 1) for i in range(planes - hop)]
        )
        down = lax.ppermute(
            down.astype(jnp.bfloat16), "outer", [(i, i - 1) for i in range(hop, planes)]
        )
    return up.astype(jnp.float32) + down.astype(jnp.float32)


def on_device(hidden_in, context, w_out, norm_gain, expert_ids, route_weight, w_gate_up, w_down):
    tok_count, width = hidden_in.shape
    planes = lax.axis_size("outer")
    zi, yi = lax.axis_index("outer"), lax.axis_index("inner")
    xi, ci = lax.axis_index("pair"), lax.axis_index("core")
    capacity = tok_count * expert_ids.shape[1] * 9 // (8 * planes * 8)
    rounds = min(planes, 8)
    group = planes // rounds
    rows = group * capacity

    spots = (zi, yi, xi, ci)
    projected, tables = project(
        context,
        w_out,
        expert_ids,
        route_weight,
        spots,
        lambda table: routing_tables(table, spots, capacity, rounds),
    )
    parts = (tables[:4], tables[4:])
    residual = hidden_in.astype(jnp.float32) + projected
    attended = residual.astype(jnp.bfloat16)
    inverse = lax.rsqrt(jnp.mean(residual * residual, axis=1, keepdims=True) + 1e-06)
    normed = (residual * inverse * norm_gain[None, :]).astype(jnp.bfloat16)

    gather = PlaneGather(normed, zi)
    across, out = [None] * rounds, [None] * rounds
    leaving = [[None, None] for _ in range(rounds)]
    came = [[None, None] for _ in range(rounds)]
    ours = [[None, None] for _ in range(rounds)]
    line = []

    def round_block(step):
        if step == 0 and planes > 1:
            gather.start()
        while len(gather.blocks) < (step + 1) * group:
            ahead = len(gather.blocks) // group - (1 if group == 1 else 2)
            gather.finish(*([across[ahead]] if ahead >= 0 else []))
            if len(gather.blocks) < planes:
                gather.start()
        blocks = gather.blocks[step * group : (step + 1) * group]
        return blocks[0] if group == 1 else jnp.concatenate(blocks)

    def pick_rows(step, part, tokens):
        pick_kept, pick_sent = parts[part][0][step], parts[part][1][step]
        got = swap(dot(pick_sent, tokens).astype(jnp.bfloat16), "core")
        kept = dot(pick_kept, tokens).astype(jnp.bfloat16)
        got, kept, *_ = lax.optimization_barrier((got, kept, *line[-LAG : len(line) - LAG + 1]))
        ours[step][part] = [kept[:rows], got[:rows]]
        leaving[step][part] = jnp.concatenate([kept[rows:], got[rows:]])
        came[step][part] = swap(leaving[step][part], "inner")
        line.append(came[step][part])

    def expert(step):
        others = [out[step - 1][1]] if step else []
        if step + 1 < rounds:
            others.append(leaving[step + 1][1])
        theirs = jnp.concatenate(came[step])
        theirs = after(theirs, *others) if others else theirs
        own = jnp.concatenate(ours[step][0] + ours[step][1])
        out[step] = expert_block(own, theirs, w_gate_up, w_down)

    for step in range(rounds + 1):
        if step < rounds:
            block = round_block(step)
            across[step] = swap(block, "pair")
        if step:
            pick_rows(step - 1, 1, across[step - 1])
        if step < rounds:
            pick_rows(step, 0, block)
            across[step] = after(across[step], leaving[step][0])
        if step > 1:
            expert(step - 2)
            if step < rounds:
                across[step] = after(across[step], out[step - 2][1])
    expert(rounds - 1)

    pieces = [None] * planes
    line = []
    crossed = sent = ahead = None
    for step in range(rounds - 1, -1, -1):
        own, theirs = out[step]
        results = [None, None]
        for part in (1, 0):
            span = slice(2 * rows * part, 2 * rows * (part + 1))
            mine, back = own[span], theirs[span]
            if step == 1 and not part:
                ahead = swap(after(out[0][1][2 * rows :], line[-1]), "inner")
                line.append(ahead)
            if ahead is not None and step == 0 and part:
                back = ahead
            else:
                back = swap(after(back, *line[-1:]) if line else back, "inner")
                line.append(back)
            back = back if sent is None else after(back, sent)
            got = swap(jnp.concatenate([mine[rows:], back[rows:]]), "core")
            results[part] = jnp.concatenate([mine[:rows], back[:rows], got])
            if part:
                if crossed is not None:
                    results[part] = after(results[part], crossed)
                high, low = parts[part][2][step], parts[part][3][step]
                sent = (dot(high, results[part]) + dot(low, results[part])).astype(jnp.bfloat16)
                crossed = swap(sent, "pair")
        high, low = parts[0][2][step], parts[0][3][step]
        piece = dot(high, results[0]) + dot(low, results[0]) + crossed.astype(jnp.float32)
        piece = piece.reshape(group, tok_count, width)
        for j in range(group):
            pieces[step * group + j] = piece[j]
    total = residual + pieces[0] + scatter_planes(pieces, zi)
    return attended, total.astype(jnp.bfloat16)


def solution(mesh):
    experts, tensors = mesh.shape["expert"], mesh.shape["tensor"]
    split = Mesh(
        mesh.devices.reshape(experts // 2, 2, tensors // 2, 2), ("outer", "inner", "pair", "core")
    )
    expert, tensor = ("outer", "inner"), ("pair", "core")
    every = expert + tensor
    in_specs = (
        P(every, None),
        P(expert, tensor),
        P(tensor, expert),
        P(),
        P(every, None),
        P(every, None),
        P(every, None, None),
        P(every, None, None),
    )
    out_specs = (P(every, None), P(every, None))
    return jax.shard_map(
        on_device, mesh=split, in_specs=in_specs, out_specs=out_specs, check_vma=False
    )
```

```python
import functools

import jax
import jax.numpy as jnp
from jax import lax
from jax.experimental import pallas as pl
from jax.experimental.pallas import tpu as pltpu
from jax.sharding import Mesh, PartitionSpec as P

SWAP = [(0, 1), (1, 0)]
LAG = 1


def swap(array, axis):
    return lax.ppermute(array, axis, SWAP)


def dot(a, b):
    return jnp.dot(a, b, preferred_element_type=jnp.float32)


def after(array, *others):
    return lax.optimization_barrier((array, *others))[0]


def plane_order(planes):
    order = []
    for plane in range(planes):
        hops = [s - plane for s in range(planes) if s != plane]
        order.append(sorted(hops, key=lambda hop: (abs(hop), hop * (-1) ** plane)))
    return order


class PlaneGather:
    def __init__(self, block, zi):
        self.planes = lax.axis_size("outer")
        self.order = plane_order(self.planes)
        self.zi, self.hop = zi, 0
        self.up = self.down = block
        self.came, self.blocks = {}, [block]

    def start(self):
        self.hop += 1
        hop, planes = self.hop, self.planes
        self.up = lax.ppermute(self.up, "outer", [(i, i + 1) for i in range(hop - 1, planes - 1)])
        self.down = lax.ppermute(
            self.down, "outer", [(i, i - 1) for i in range(1, planes - hop + 1)]
        )

    def finish(self, *others):
        self.up, self.down, *_ = lax.optimization_barrier((self.up, self.down, *others))
        self.came[-self.hop], self.came[self.hop] = self.up, self.down
        hops = [self.order[plane][self.hop - 1] for plane in range(self.planes)]
        chosen = None
        for hop in sorted(set(hops)):
            if chosen is None:
                chosen = self.came[hop]
            else:
                here = jnp.zeros((), bool)
                for plane in range(self.planes):
                    if hops[plane] == hop:
                        here = here | (self.zi == plane)
                chosen = jnp.where(here, self.came[hop], chosen)
        self.blocks.append(chosen)


def project(context, w_out, expert_ids, route_weight, spots, make_tables):
    zi, yi, xi, ci = spots
    planes = lax.axis_size("outer")
    rows, depth = context.shape
    tok_count = rows // 4
    columns = PlaneGather(w_out, zi)
    columns.start()
    other_rows = swap(context, "inner")
    table = jnp.concatenate([expert_ids.T.astype(jnp.float32), route_weight.T])
    table = jnp.stack([table, swap(table, "pair")])
    order = plane_order(planes)
    table = after(table, other_rows)
    by_offset = [table] + [
        lax.ppermute(table, "outer", [(i, i ^ offset) for i in range(planes)])
        for offset in range(1, planes)
    ]
    near = [[plane ^ (plane + hop) for hop in [0] + order[plane]] for plane in range(planes)]
    tables = make_tables(jnp.take(jnp.stack(by_offset), jnp.array(near)[zi], axis=0))
    both = jnp.stack([context, other_rows]).reshape(2, 2, 2, tok_count, depth)
    theirs = lax.dynamic_index_in_dim(both, 1 - ci, 2, keepdims=False).reshape(-1, depth)
    mine = lax.dynamic_index_in_dim(both, ci, 2, keepdims=False).reshape(-1, depth)
    parts, crossing = [], []
    for step in range(planes):
        if step:
            gates = list(crossing[:2] if step == 2 else crossing[step - 1 :] if step > 2 else [])
            if step == min(2, planes - 1):
                gates += tables
            columns.finish(*gates)
            if step + 1 < planes:
                columns.start()
        weights = columns.blocks[step]
        sent = dot(theirs, weights).astype(jnp.bfloat16)
        kept = dot(mine, weights) + swap(sent, "core").astype(jnp.float32)
        kept = kept.reshape(2, 2, tok_count, -1)
        sent = lax.dynamic_index_in_dim(kept, 1 - xi, 1, keepdims=False).astype(jnp.bfloat16)
        crossing.append(sent)
        kept = lax.dynamic_index_in_dim(kept, xi, 1, keepdims=False)
        kept = kept + swap(sent, "pair").astype(jnp.float32)
        other = swap(kept[1].astype(jnp.bfloat16), "inner").astype(jnp.float32)
        low = jnp.where(yi == 0, kept[0], other)
        high = jnp.where(yi == 0, other, kept[0])
        parts.append(jnp.concatenate([low, high], axis=1))
    where = [
        [([0] + order[plane]).index(target - plane) for target in range(planes)]
        for plane in range(planes)
    ]
    where = jnp.array(where)[zi]
    parts = jnp.stack(parts)
    projected = jnp.concatenate(
        [lax.dynamic_index_in_dim(parts, where[p], 0, keepdims=False) for p in range(planes)], axis=1
    )
    return projected, tables


def routing_tables(table, spots, capacity, rounds):
    zi, yi, xi, ci = spots
    planes, _, top_count, tok_count = table.shape
    top_count //= 2
    group = planes // rounds
    rows = group * capacity
    table = table.reshape(rounds, group, 2, -1, tok_count)
    chosen, weight = [], []
    for core in range(2):
        for side in range(2):
            expert = ((zi * 2 + (yi ^ side)) * 2 + xi) * 2 + (ci ^ core)
            named = table[..., :top_count, :] == expert.astype(jnp.float32)
            chosen.append(jnp.any(named, axis=3))
            weight.append(jnp.sum(jnp.where(named, table[..., top_count:, :], 0.0), axis=3))
    chosen, weight = jnp.stack(chosen), jnp.stack(weight)
    earlier = jnp.arange(tok_count)[:, None] < jnp.arange(tok_count)[None, :]
    slots = dot(chosen.astype(jnp.bfloat16), earlier.astype(jnp.bfloat16)).astype(jnp.int32)
    first = jnp.arange(4)[:, None, None, None, None] * rows
    first = first + jnp.arange(group)[None, None, :, None, None] * capacity
    row = jnp.where(chosen, slots + first, -1)
    order = (3, 0, 1, 2, 4)
    row = row.transpose(order).reshape(2, 4, rounds, -1)
    weight = weight.transpose(order).reshape(2, 4, rounds, -1)
    parts = []
    for part in range(2):
        own, theirs, other, diagonal = (row[part, i, :, None, :] for i in range(4))
        spot = jnp.arange(2 * rows)[None, :, None]
        kept = (own == spot) | (theirs == spot)
        spot = spot + 2 * rows
        sent = (other == spot) | (diagonal == spot)
        spread = 0.0
        for i in range(4):
            here = row[part, i, :, :, None] == jnp.arange(4 * rows)
            spread = spread + jnp.where(here, weight[part, i, :, :, None], 0.0)
        high = spread.astype(jnp.bfloat16)
        low = (spread - high.astype(jnp.float32)).astype(jnp.bfloat16)
        parts += [kept.astype(jnp.bfloat16), sent.astype(jnp.bfloat16), high, low]
    return lax.optimization_barrier(tuple(parts))


def expert_kernel(steps, own, theirs, gate, up, down, own_out, theirs_out, tokens, total):
    step = pl.program_id(0)
    rows = own.shape[0]

    @pl.when(step == 0)
    def _():
        tokens[:rows, :] = own[...]
        tokens[rows:, :] = theirs[...]

    gated = dot(tokens[...], gate[0])
    act = gated / (1.0 + jnp.exp(-gated)) * dot(tokens[...], up[0])
    part = dot(act.astype(jnp.bfloat16), down[0])

    @pl.when(step == 0)
    def _():
        total[...] = part

    @pl.when(step > 0)
    def _():
        total[...] += part

    @pl.when(step == steps - 1)
    def _():
        own_out[...] = total[:rows, :].astype(jnp.bfloat16)
        theirs_out[...] = total[rows:, :].astype(jnp.bfloat16)


def expert_block(own, theirs, w_gate_up, w_down):
    rows, width = own.shape
    hidden_units = w_down.shape[1]
    tile = 256 if hidden_units % 256 == 0 else 128
    steps = hidden_units // tile
    whole = pl.BlockSpec((rows, width), lambda i: (0, 0))
    return pl.pallas_call(
        functools.partial(expert_kernel, steps),
        grid=(steps,),
        in_specs=[
            whole,
            whole,
            pl.BlockSpec((1, width, tile), lambda i: (0, 0, i)),
            pl.BlockSpec((1, width, tile), lambda i: (0, 0, i + steps)),
            pl.BlockSpec((1, tile, width), lambda i: (0, i, 0)),
        ],
        out_specs=[whole, whole],
        out_shape=[jax.ShapeDtypeStruct((rows, width), jnp.bfloat16)] * 2,
        scratch_shapes=[
            pltpu.VMEM((2 * rows, width), jnp.bfloat16),
            pltpu.VMEM((2 * rows, width), jnp.float32),
        ],
        compiler_params=pltpu.CompilerParams(vmem_limit_bytes=44 * 2**20),
        cost_estimate=pl.CostEstimate(flops=1, bytes_accessed=1, transcendentals=0),
    )(own, theirs, w_gate_up, w_gate_up, w_down)


def scatter_planes(pieces, zi):
    planes = lax.axis_size("outer")
    order = plane_order(planes)

    def piece(hop):
        chosen = None
        for step in range(planes - 1):
            here = [plane for plane in range(planes) if order[plane][step] == hop]
            if not here:
                continue
            if chosen is None:
                chosen = pieces[step + 1]
            else:
                at = jnp.zeros((), bool)
                for plane in here:
                    at = at | (zi == plane)
                chosen = jnp.where(at, pieces[step + 1], chosen)
        return chosen

    up = down = None
    for hop in range(planes - 1, 0, -1):
        up = piece(hop) if up is None else piece(hop) + up.astype(jnp.float32)
        down = piece(-hop) if down is None else piece(-hop) + down.astype(jnp.float32)
        up, down = up.astype(jnp.bfloat16), down.astype(jnp.bfloat16)
        if hop > 1:
            up = lax.ppermute(up, "outer", [(i, i + 1) for i in range(planes - hop)])
            down = lax.ppermute(down, "outer", [(i, i - 1) for i in range(hop, planes)])
    even = zi % 2 == 0
    total = 0.0
    for link, sent in ((1, jnp.where(even, down, up)), (0, jnp.where(even, up, down))):
        low = range(link, planes - 1, 2)
        pairs = [(i, i + 1) for i in low] + [(i + 1, i) for i in low]
        if pairs:
            total = total + lax.ppermute(sent, "outer", pairs).astype(jnp.float32)
    return total


def on_device(hidden_in, context, w_out, norm_gain, expert_ids, route_weight, w_gate_up, w_down):
    tok_count, width = hidden_in.shape
    planes = lax.axis_size("outer")
    zi, yi = lax.axis_index("outer"), lax.axis_index("inner")
    xi, ci = lax.axis_index("pair"), lax.axis_index("core")
    capacity = tok_count * expert_ids.shape[1] * 9 // (8 * planes * 8)
    rounds = min(planes, 8)
    group = planes // rounds
    rows = group * capacity

    spots = (zi, yi, xi, ci)
    projected, tables = project(
        context,
        w_out,
        expert_ids,
        route_weight,
        spots,
        lambda table: routing_tables(table, spots, capacity, rounds),
    )
    parts = (tables[:4], tables[4:])
    residual = hidden_in.astype(jnp.float32) + projected
    attended = residual.astype(jnp.bfloat16)
    inverse = lax.rsqrt(jnp.mean(residual * residual, axis=1, keepdims=True) + 1e-06)
    normed = (residual * inverse * norm_gain[None, :]).astype(jnp.bfloat16)

    gather = PlaneGather(normed, zi)
    across, out = [None] * rounds, [None] * rounds
    leaving = [[None, None] for _ in range(rounds)]
    came = [[None, None] for _ in range(rounds)]
    ours = [[None, None] for _ in range(rounds)]
    line = []

    def round_block(step):
        if step == 0 and planes > 1:
            gather.start()
        while len(gather.blocks) < (step + 1) * group:
            ahead = len(gather.blocks) // group - (1 if group == 1 else 2)
            gather.finish(*([across[ahead]] if ahead >= 0 else []))
            if len(gather.blocks) < planes:
                gather.start()
        blocks = gather.blocks[step * group : (step + 1) * group]
        return blocks[0] if group == 1 else jnp.concatenate(blocks)

    def pick_rows(step, part, tokens):
        pick_kept, pick_sent = parts[part][0][step], parts[part][1][step]
        got = swap(dot(pick_sent, tokens).astype(jnp.bfloat16), "core")
        kept = dot(pick_kept, tokens).astype(jnp.bfloat16)
        got, kept, *_ = lax.optimization_barrier((got, kept, *line[-LAG : len(line) - LAG + 1]))
        ours[step][part] = [kept[:rows], got[:rows]]
        leaving[step][part] = jnp.concatenate([kept[rows:], got[rows:]])
        came[step][part] = swap(leaving[step][part], "inner")
        line.append(came[step][part])

    def expert(step):
        others = [out[step - 1][1]] if step else []
        if step + 1 < rounds:
            others.append(leaving[step + 1][1])
        theirs = jnp.concatenate(came[step])
        theirs = after(theirs, *others) if others else theirs
        own = jnp.concatenate(ours[step][0] + ours[step][1])
        out[step] = expert_block(own, theirs, w_gate_up, w_down)

    for step in range(rounds + 1):
        if step < rounds:
            block = round_block(step)
            across[step] = swap(block, "pair")
        if step:
            pick_rows(step - 1, 1, across[step - 1])
        if step < rounds:
            pick_rows(step, 0, block)
            across[step] = after(across[step], leaving[step][0])
        if step > 1:
            expert(step - 2)
            if step < rounds:
                across[step] = after(across[step], out[step - 2][1])
    expert(rounds - 1)

    pieces = [None] * planes
    line = []
    crossed = sent = ahead = None
    for step in range(rounds - 1, -1, -1):
        own, theirs = out[step]
        results = [None, None]
        for part in (1, 0):
            span = slice(2 * rows * part, 2 * rows * (part + 1))
            mine, back = own[span], theirs[span]
            if step == 1 and not part:
                ahead = swap(after(out[0][1][2 * rows :], line[-1]), "inner")
                line.append(ahead)
            if ahead is not None and step == 0 and part:
                back = ahead
            else:
                back = swap(after(back, *line[-1:]) if line else back, "inner")
                line.append(back)
            back = back if sent is None else after(back, sent)
            got = swap(jnp.concatenate([mine[rows:], back[rows:]]), "core")
            results[part] = jnp.concatenate([mine[:rows], back[:rows], got])
            if part:
                if crossed is not None:
                    results[part] = after(results[part], crossed)
                high, low = parts[part][2][step], parts[part][3][step]
                sent = (dot(high, results[part]) + dot(low, results[part])).astype(jnp.bfloat16)
                crossed = swap(sent, "pair")
        high, low = parts[0][2][step], parts[0][3][step]
        piece = dot(high, results[0]) + dot(low, results[0]) + crossed.astype(jnp.float32)
        piece = piece.reshape(group, tok_count, width)
        for j in range(group):
            pieces[step * group + j] = piece[j]
    total = residual + pieces[0] + scatter_planes(pieces, zi)
    return attended, total.astype(jnp.bfloat16)


def solution(mesh):
    experts, tensors = mesh.shape["expert"], mesh.shape["tensor"]
    split = Mesh(
        mesh.devices.reshape(experts // 2, 2, tensors // 2, 2), ("outer", "inner", "pair", "core")
    )
    expert, tensor = ("outer", "inner"), ("pair", "core")
    every = expert + tensor
    in_specs = (
        P(every, None),
        P(expert, tensor),
        P(tensor, expert),
        P(),
        P(every, None),
        P(every, None),
        P(every, None, None),
        P(every, None, None),
    )
    out_specs = (P(every, None), P(every, None))
    return jax.shard_map(
        on_device, mesh=split, in_specs=in_specs, out_specs=out_specs, check_vma=False
    )
```
